512 devices in a mesh: ctx: 128 (over y, z, core), req: 4 (over x).
Axes of the slice: x: 4, y: 8, z: 8, core: 2. Of those that a mesh axis runs over, the one named last changes fastest.
Arguments:
- queries: bfloat16 [65536, 1024], P(('req', 'ctx')), parts along dimension 0, may hold values from -6 to 6
- keys: bfloat16 [65536, 256], P(('req', 'ctx')), parts along dimension 0, may hold values from -6 to 6
- lse: float32 [16, 65536], P(None, ('req', 'ctx')), parts along dimension 1, may hold values from -0.5 to 15, as said below
- length: int32 [4], P('req'), parts along dimension 0, may hold values from 8192 to 16384
Outputs:
- key_scores: float32 [16, 65536], P(None, ('req', 'ctx')), parts along dimension 1
The draws below stay inside these ranges and needn't reach their ends.
There are 4 independent parts, one for each index of `req`. The reference program is written for one: setup_inputs(seed, part) draws one part's arguments, and reference() takes and returns one part's arrays. A program takes and returns all parts, laid end to end along the dimension named above; each array names one. Nothing has to cross between parts.
Inputs may be any that keep to these rules, and one draw needn't show every extreme that they name: lse[h, i] is the logarithm of i + 1 plus an offset between -0.5 and 3.
All inputs are finite; a program needn't handle non-finite values.
Results may differ from the reference program's by a relative error of at most 0.0003.
Values may be sent and summed in bfloat16 or wider, within the bound.
A program may use at most 64 MiB of HBM per device.

```python
import math
import jax
import jax.numpy as jnp
from jax import lax

HEADS = 16
KV_HEADS = 4
HEAD_DIM = 64
TOKENS = 16384


def draw_lse(key, part):
    position = jnp.arange(TOKENS, dtype=jnp.float32)
    offset = jax.random.uniform(key, (HEADS, TOKENS), jnp.float32, 0.0, 2.0)
    return jnp.log(position + 1.0)[None, :] + offset


def steps_of(own_key, dims, cuts, low, high):
    level, own = 1.0, jax.random.fold_in(own_key, 6)
    for axis_at, parts in cuts:
        steps = jnp.exp(jax.random.uniform(jax.random.fold_in(own, axis_at), (parts,), jnp.float32, low / len(cuts), high / len(cuts)))
        level = level * jnp.repeat(steps, dims[axis_at] // parts).reshape([-1 if axis == axis_at else 1 for axis in range(len(dims))])
    return level


def centred(rng, shape, spread, most, cuts=(), kind=jnp.bfloat16):
    entries = spread * jax.random.normal(rng, shape, jnp.float32)
    if cuts:
        entries = entries * steps_of(rng, shape, cuts, -0.22, 0.18)
    return jnp.clip(entries, -most, most).astype(kind)


def setup_inputs(seed: int = 0, part: int = 0) -> dict:
    arg_keys = jax.random.split(jax.random.key(seed), 5)
    own_keys = jax.random.split(jax.random.fold_in(arg_keys[4], part), 5)
    return {
        "queries": centred(own_keys[0], (TOKENS, HEADS * HEAD_DIM), 1.0, 6.0, ((0, 128),)),
        "keys": centred(own_keys[1], (TOKENS, KV_HEADS * HEAD_DIM), 1.0, 6.0, ((0, 128),)),
        "lse": draw_lse(jax.random.fold_in(jax.random.fold_in(arg_keys[4], part), 71), part),
        "length": jax.random.randint(own_keys[3], (1,), TOKENS // 2, TOKENS + 1).astype(jnp.int32),
    }


def reference(queries, keys, lse, length):
    limit = length[0]
    positions = jnp.arange(TOKENS, dtype=jnp.int32)
    block_len = math.gcd(TOKENS, 256)
    group = HEADS // KV_HEADS
    grouped = queries.astype(jnp.float32).reshape(TOKENS, KV_HEADS, group, HEAD_DIM)

    def one_block(index):
        key_start = (index * block_len).astype(jnp.int32)
        key_block = lax.dynamic_slice_in_dim(keys, key_start, block_len, 0)
        key_view = key_block.astype(jnp.float32).reshape(block_len, KV_HEADS, HEAD_DIM)
        logits = jnp.einsum("rhgd,chd->hgrc", grouped, key_view).reshape(HEADS, TOKENS, block_len) * (HEAD_DIM ** -0.5)
        key_pos = key_start + jnp.arange(block_len, dtype=jnp.int32)
        valid = (positions[:, None] >= key_pos[None, :]) & (positions[:, None] < limit)
        weights = jnp.where(valid[None], jnp.exp(logits - lse[:, :, None]), jnp.float32(0.0))
        return jnp.sum(weights, axis=1)

    blocks = lax.map(one_block, jnp.arange(TOKENS // block_len, dtype=jnp.int32))
    return jnp.transpose(blocks, (1, 0, 2)).reshape(HEADS, TOKENS)
```

```python
import functools

import jax
import jax.numpy as jnp
from jax import lax
from jax.experimental import pallas as pl
from jax.experimental.pallas import tpu as pltpu
from jax.sharding import PartitionSpec as P

HEAD_DIM = 64
TOK = 128
NY, NZ = 8, 8
GROUP = 4
PAST = -30000.0
F32, BF16 = jnp.float32, jnp.bfloat16


def member(half, index):
    return 2 * index + (half + index // 2) % 2


def kernel(
    len_ref, q_ref, k_ref, l_ref, o_ref,
    qsend, kpack, kbuf, qbuf, qaug, kaug, acc, part, abuf, ssum, bbuf,
    col_s, col_r, q_s, q_r, relay_s, relay_r, ring_s, ring_r, a_s, a_r, b_s, b_r,
):
    me = lax.axis_index("ctx")
    y, z, c = me // 16, (me // 2) % 8, me % 2
    half, mine = (y + y // 4) % 2, y // 2

    def device(ty, tz, tc):
        return {"ctx": ty * 16 + tz * 2 + tc}

    def remote(src, dst, send, recv, dev):
        return pltpu.make_async_remote_copy(
            src_ref=src, dst_ref=dst, send_sem=send, recv_sem=recv, device_id=dev
        )

    barrier = pltpu.get_barrier_semaphore()

    def greet(dev):
        pl.semaphore_signal(barrier, inc=1, device_id=dev)

    greet(device(y, z, 1 - c))
    for step in range(1, 8):
        greet(device((y + step) % 8, z, c))
        greet(device(y, (z + step) % 8, c))

    lane64 = lax.broadcasted_iota(jnp.int32, (64, TOK), 1)

    for pair in range(2):
        two = k_ref[:, pair * 128 : pair * 128 + 128].astype(F32) * HEAD_DIM**-0.5
        top, low = two[:64], two[64:]
        top_r, low_r = pltpu.roll(top, 64, 1), pltpu.roll(low, 64, 1)
        kpack[2 * pair] = jnp.where(lane64 < 64, top, low_r).astype(BF16)
        kpack[2 * pair + 1] = jnp.where(lane64 < 64, top_r, low).astype(BF16)
    kbuf[z, y] = kpack[mine]

    position = me * TOK + lax.broadcasted_iota(jnp.int32, (16, TOK), 1)
    neg = jnp.where(position < len_ref[0], -l_ref[...], PAST)
    hi = neg.astype(BF16).astype(F32)
    mid = (neg - hi).astype(BF16).astype(F32)
    low = neg - hi - mid
    for head in range(4):
        rows = slice(4 * head, 4 * head + 4)
        parts = jnp.concatenate(
            [hi[rows], mid[rows], low[rows], jnp.zeros((4, TOK), F32)], axis=0
        )
        qsend[head, :TOK, :] = q_ref[:, head * 256 : head * 256 + 256]
        qsend[head, TOK:, :] = jnp.concatenate([parts, parts], axis=1).astype(BF16)

    pl.semaphore_wait(barrier, 15)

    def column(src_y, dst_y):
        return remote(
            kpack.at[dst_y // 2], kbuf.at[z, src_y], col_s.at[dst_y], col_r.at[src_y],
            device(dst_y, z, c),
        )

    def query(src_m, dst_m):
        return remote(
            qsend.at[dst_m], qbuf.at[src_m, c], q_s.at[dst_m], q_r.at[src_m],
            device(member(half, dst_m), z, c),
        )

    def relay(src, m, core):
        return remote(src, qbuf.at[m, core], relay_s.at[m], relay_r.at[m], device(y, z, 1 - c))

    def ring(way, dist, part_of):
        sign = 1 - 2 * way
        block = (z - sign * (dist - 1)) % 8
        where = kbuf.at[block, pl.ds(4 * part_of, 4)]
        return remote(
            where, where, ring_s.at[way, dist - 1, part_of], ring_r.at[way, dist - 1, part_of],
            device(y, (z + sign) % 8, c),
        )

    for step in range(1, 8):
        column(y, (y + step) % 8).start()
    own = relay(qsend.at[mine], mine, c)
    own.start()
    for step in range(1, 4):
        query(mine, (mine + step) % 4).start()
    qbuf[mine, c] = qsend[mine]

    for part_of in range(2):
        for src in range(4 * part_of, 4 * part_of + 4):

            @pl.when(src != y)
            def _():
                column(src, y).wait_recv()

        for way in range(2):
            ring(way, 1, part_of).start()

    def advance(dist):
        for part_of in range(2):
            for way in range(2):
                ring(way, dist, part_of).wait_recv()
                if dist < 3 or part_of == way:
                    ring(way, dist + 1, part_of).start()

    for step in range(1, 4):
        src = (mine - step) % 4
        query(src, mine).wait_recv()
        relay(qbuf.at[src, c], src, c).start()
    advance(1)
    for step in range(4):
        m = (mine - step) % 4
        relay(qbuf.at[m, 1 - c], m, 1 - c).wait_recv()

    lane = lax.broadcasted_iota(jnp.int32, (TOK, TOK), 1)

    def prepare(index, carry):
        m, core = index // 2, index % 2
        tail = qbuf[m, core, TOK:, :TOK].astype(F32)
        cols = jnp.concatenate(
            [jnp.zeros((64, TOK), F32), tail, jnp.zeros((48, TOK), F32)], axis=0
        ).T
        for pair in range(2):
            two = qbuf[m, core, :TOK, pair * 128 : pair * 128 + 128].astype(F32)
            for odd in range(2):
                g = 2 * pair + odd
                head = pltpu.roll(two, 64, 1) if odd else two
                keep = (lane >= 64) & (lane % 4 == g)
                value = jnp.where(lane < 64, head, jnp.where(keep, cols, 0.0))
                qaug[m, g, pl.ds(core * TOK, TOK), :] = value.astype(BF16)
        return carry

    lax.fori_loop(0, 8, prepare, 0)
    advance(2)

    tokens = lax.broadcasted_iota(jnp.int32, (2 * TOK, TOK), 0)
    key_at = lax.broadcasted_iota(jnp.int32, (2 * TOK, TOK), 1) + c * TOK

    def tile(m, start, width, masked=False):
        keys = kaug[pl.ds(start, width), :]
        for g in range(4):
            s = lax.dot_general(
                qaug[m, g], keys, (((1,), (1,)), ((), ())), preferred_element_type=F32
            )
            w = jnp.exp(s)
            if masked:
                w = jnp.where(tokens >= key_at, w, 0.0)
            acc[g, :, pl.ds(start, width)] += jnp.sum(w.reshape(-1, 8, width), axis=0)

    def block_at(turn):
        sign = 1 - 2 * (turn % 2)
        away = jnp.where(turn == 7, 0, (turn // 2 + 1) * sign)
        return (z - away + 8) % 8

    def to_row_mate(block):
        return remote(
            part.at[block], abuf.at[z], a_s.at[block], a_r.at[z], device(y, block, c)
        )

    def one_block(turn, carry):
        block = block_at(turn)

        @pl.when(turn == 3)
        def _():
            advance(3)

        @pl.when(turn == 6)
        def _():
            for way in range(2):
                ring(way, 4, way).wait_recv()

        for src in range(8):
            packed = kbuf[block, src].astype(F32)
            tail = jnp.where(lane64 < 76, 1.0, 0.0)
            kaug[src * TOK : src * TOK + 64, :] = jnp.where(lane64 < 64, packed, tail).astype(BF16)
            kaug[src * TOK + 64 : src * TOK + 128, :] = jnp.where(
                lane64 < 64, pltpu.roll(packed, 64, 1), tail
            ).astype(BF16)
        acc[...] = jnp.zeros_like(acc)
        for m in range(1, 4):
            tile(m, 0, 256 * m)
        odd_m, even_m = 2 * (1 - half), 2 * half

        def at(m, add):
            return pl.multiple_of(256 * m + add, 128)

        @pl.when(block < z)
        def _():
            for i in range(2):
                tile(odd_m + i, at(odd_m + i, 0), 256)
                tile(even_m + i, at(even_m + i, 0), 128)

        @pl.when(block >= z)
        def _():
            for i in range(2):
                tile(odd_m + i, at(odd_m + i, 0), 128)

        @pl.when(block == z)
        def _():
            for i in range(2):
                tile(odd_m + i, at(odd_m + i, 128), 128, masked=True)
                tile(even_m + i, at(even_m + i, 0), 128, masked=True)

        rows = [jnp.sum(acc[g], axis=0, keepdims=True) for g in range(4)]
        part[block] = jnp.concatenate(
            [r[:, :512] for r in rows] + [r[:, 512:] for r in rows], axis=0
        )

        @pl.when(turn < 7)
        def _():
            to_row_mate(block).start()

        return carry

    lax.fori_loop(0, 8, one_block, 0)

    total = part[z]
    for step in range(1, 8):
        src = (z + step) % 8
        remote(part.at[z], abuf.at[src], a_s.at[src], a_r.at[src], device(y, src, c)).wait_recv()
        total += abuf[src]
    for i in range(4):
        ssum[i] = total[:, i * 128 : i * 128 + 128]

    def to_owner(src_y, dst_y):
        return remote(
            ssum.at[dst_y % 4], bbuf.at[src_y], b_s.at[dst_y], b_r.at[src_y],
            device(dst_y, z, c),
        )

    for step in range(1, 8):
        to_owner(y, (y + step) % 8).start()
    bbuf[y] = ssum[y % 4]

    for step in range(1, 8):
        column(y, (y + step) % 8).wait_send()
        to_row_mate((z + step) % 8).wait_send()
    for step in range(1, 4):
        query(mine, (mine + step) % 4).wait_send()
    for m in range(4):
        relay(qbuf.at[m, c], m, c).wait_send()
    for way in range(2):
        for dist in range(1, 5):
            for part_of in range(2):
                if dist < 4 or part_of == way:
                    ring(way, dist, part_of).wait_send()

    for step in range(1, 8):
        to_owner((y + step) % 8, y).wait_recv()
    for h in range(4):
        both = bbuf[2 * h] + bbuf[2 * h + 1]
        o_ref[4 * h : 4 * h + 4, :] = jnp.where(y // 4 == 0, both[:4], both[4:])
    for step in range(1, 8):
        to_owner(y, (y + step) % 8).wait_send()


def shard(queries, keys, lse, length):
    vmem = pl.BlockSpec(memory_space=pltpu.VMEM)
    dma = pltpu.SemaphoreType.DMA
    return pl.pallas_call(
        kernel,
        out_shape=jax.ShapeDtypeStruct(lse.shape, F32),
        in_specs=[pl.BlockSpec(memory_space=pltpu.SMEM), vmem, vmem, vmem],
        out_specs=vmem,
        scratch_shapes=[
            pltpu.VMEM((4, TOK + 16, 256), BF16),
            pltpu.VMEM((4, 64, 128), BF16),
            pltpu.VMEM((NZ, NY, 64, 128), BF16),
            pltpu.VMEM((4, 2, TOK + 16, 256), BF16),
            pltpu.VMEM((4, 4, 2 * TOK, 128), BF16),
            pltpu.VMEM((NY * TOK, 128), BF16),
            pltpu.VMEM((4, 8, NY * TOK), F32),
            pltpu.VMEM((NZ, 8, 512), F32),
            pltpu.VMEM((NZ, 8, 512), F32),
            pltpu.VMEM((4, 8, 128), F32),
            pltpu.VMEM((NY, 8, 128), F32),
            dma((8,)), dma((8,)), dma((4,)), dma((4,)), dma((4,)), dma((4,)),
            dma((2, 4, 2)), dma((2, 4, 2)), dma((8,)), dma((8,)), dma((8,)), dma((8,)),
        ],
        compiler_params=pltpu.CompilerParams(
            collective_id=0, has_side_effects=True, vmem_limit_bytes=48 * 2**20
        ),
    )(length, queries, keys, lse)


def solution(mesh):
    both = ("req", "ctx")
    return jax.shard_map(
        shard,
        mesh=mesh,
        in_specs=(P(both, None), P(both, None), P(None, both), P("req")),
        out_specs=P(None, both),
        check_vma=False,
    )
```

```python
import functools

import jax
import jax.numpy as jnp
from jax import lax
from jax.experimental import pallas as pl
from jax.experimental.pallas import tpu as pltpu
from jax.sharding import PartitionSpec as P

HEAD_DIM = 64
TOK = 128
NY, NZ = 8, 8
GROUP = 4
PAST = -30000.0
F32, BF16 = jnp.float32, jnp.bfloat16


def member(half, index):
    return 2 * index + (half + index // 2) % 2


def kernel(
    len_ref, q_hbm, k_hbm, l_hbm, o_ref,
    q_ref, k_ref, l_ref, qsend, kpack, kbuf, qbuf, qaug, kaug, acc, part, abuf,
    in_s, col_s, col_r, q_s, q_r, relay_s, relay_r, ring_s, ring_r, a_s, a_r,
):
    me = lax.axis_index("ctx")
    y, z, c = me // 16, (me // 2) % 8, me % 2
    half, mine = (y + y // 4) % 2, y // 2

    def device(ty, tz, tc):
        return {"ctx": ty * 16 + tz * 2 + tc}

    def remote(src, dst, send, recv, dev):
        return pltpu.make_async_remote_copy(
            src_ref=src, dst_ref=dst, send_sem=send, recv_sem=recv, device_id=dev
        )

    loads = [
        pltpu.make_async_copy(src, dst, in_s.at[i])
        for i, (src, dst) in enumerate(((k_hbm, k_ref), (l_hbm, l_ref), (q_hbm, q_ref)))
    ]
    for load in loads:
        load.start()
    barrier = pltpu.get_barrier_semaphore()

    def greet(dev):
        pl.semaphore_signal(barrier, inc=1, device_id=dev)

    greet(device(y, z, 1 - c))
    for step in range(1, 8):
        greet(device((y + step) % 8, z, c))
        greet(device(y, (z + step) % 8, c))

    lane64 = lax.broadcasted_iota(jnp.int32, (64, TOK), 1)

    for load in loads:
        load.wait()

    for pair in range(2):
        two = k_ref[:, pair * 128 : pair * 128 + 128].astype(F32) * HEAD_DIM**-0.5
        top, low = two[:64], two[64:]
        top_r, low_r = pltpu.roll(top, 64, 1), pltpu.roll(low, 64, 1)
        kpack[2 * pair] = jnp.where(lane64 < 64, top, low_r).astype(BF16)
        kpack[2 * pair + 1] = jnp.where(lane64 < 64, top_r, low).astype(BF16)
    kbuf[z, y] = kpack[mine]

    position = me * TOK + lax.broadcasted_iota(jnp.int32, (16, TOK), 1)
    neg = jnp.where(position < len_ref[0], -l_ref[...], PAST)
    hi = neg.astype(BF16).astype(F32)
    mid = (neg - hi).astype(BF16).astype(F32)
    low = neg - hi - mid
    for head in range(4):
        rows = slice(4 * head, 4 * head + 4)
        parts = jnp.concatenate(
            [hi[rows], mid[rows], low[rows], jnp.zeros((4, TOK), F32)], axis=0
        )
        qsend[head, :TOK, :] = q_ref[:, head * 256 : head * 256 + 256]
        qsend[head, TOK:, :] = jnp.concatenate([parts, parts], axis=1).astype(BF16)

    pl.semaphore_wait(barrier, 15)

    def column(src_y, dst_y):
        return remote(
            kpack.at[dst_y // 2], kbuf.at[z, src_y], col_s.at[dst_y], col_r.at[src_y],
            device(dst_y, z, c),
        )

    def query(src_m, dst_m):
        return remote(
            qsend.at[dst_m], qbuf.at[src_m, c], q_s.at[dst_m], q_r.at[src_m],
            device(member(half, dst_m), z, c),
        )

    def relay(src, m, core):
        return remote(src, qbuf.at[m, core], relay_s.at[m], relay_r.at[m], device(y, z, 1 - c))

    def ring(way, dist, part_of):
        sign = 1 - 2 * way
        from_dist, hop = (2, 2) if dist == 4 else (dist - 1, 1)
        block = (z - sign * from_dist) % 8
        where = kbuf.at[block, pl.ds(4 * part_of, 4)]
        return remote(
            where, where, ring_s.at[way, dist - 1, part_of], ring_r.at[way, dist - 1, part_of],
            device(y, (z + hop * sign) % 8, c),
        )

    for step in range(1, 8):
        column(y, (y + step) % 8).start()
    own = relay(qsend.at[mine], mine, c)
    own.start()
    for step in range(1, 4):
        query(mine, (mine + step) % 4).start()
    qbuf[mine, c] = qsend[mine]

    for part_of in range(2):
        for src in range(4 * part_of, 4 * part_of + 4):

            @pl.when(src != y)
            def _():
                column(src, y).wait_recv()

        for way in range(2):
            ring(way, 1, part_of).start()

    def advance(dist):
        for part_of in range(2):
            for way in range(2):
                if dist < 4 or part_of == way:
                    ring(way, dist, part_of).wait_recv()
                if dist < 3:
                    ring(way, dist + 1, part_of).start()
                if dist == 2 and part_of == way:
                    ring(way, 4, part_of).start()

    lane = lax.broadcasted_iota(jnp.int32, (TOK, TOK), 1)

    def prepare(m, core):
        tail = qbuf[m, core, TOK:, :TOK].astype(F32)
        cols = jnp.concatenate(
            [jnp.zeros((64, TOK), F32), tail, jnp.zeros((48, TOK), F32)], axis=0
        ).T
        for pair in range(2):
            two = qbuf[m, core, :TOK, pair * 128 : pair * 128 + 128].astype(F32)
            for odd in range(2):
                g = 2 * pair + odd
                head = pltpu.roll(two, 64, 1) if odd else two
                keep = (lane >= 64) & (lane % 4 == g)
                value = jnp.where(lane < 64, head, jnp.where(keep, cols, 0.0))
                qaug[m, g, pl.ds(core * TOK, TOK), :] = value.astype(BF16)

    prepare(mine, c)
    relay(qbuf.at[mine, 1 - c], mine, 1 - c).wait_recv()
    prepare(mine, 1 - c)
    for step in range(1, 4):
        src = (mine - step) % 4
        query(src, mine).wait_recv()
        relay(qbuf.at[src, c], src, c).start()
        prepare(src, c)
    advance(1)
    for step in range(1, 4):
        src = (mine - step) % 4
        relay(qbuf.at[src, 1 - c], src, 1 - c).wait_recv()
        prepare(src, 1 - c)

    tokens = lax.broadcasted_iota(jnp.int32, (2 * TOK, 2 * TOK), 0)
    key_of = lax.broadcasted_iota(jnp.int32, (1, 2 * TOK), 1)

    def compute(block):
        for src in range(8):
            packed = kbuf[block, src].astype(F32)
            tail = jnp.where(lane64 < 76, 1.0, 0.0)
            at = src * TOK
            kaug[at : at + 64, :] = jnp.where(lane64 < 64, packed, tail).astype(BF16)
            kaug[at + 64 : at + 128, :] = jnp.where(
                lane64 < 64, pltpu.roll(packed, 64, 1), tail
            ).astype(BF16)
        for m in range(3, -1, -1):
            width = 256 * (m + 1)
            key_at = ((2 * m + key_of // TOK) * NZ + block) * 2 * TOK + c * TOK + key_of % TOK
            first = key_at - (member(half, m) * NZ + z) * 2 * TOK
            for g in range(4):
                w = jnp.exp(
                    lax.dot_general(
                        qaug[m, g], kaug[:width, :], (((1,), (1,)), ((), ())),
                        preferred_element_type=F32,
                    )
                )
                seen = jnp.where(tokens >= first, w[:, width - 256 :], 0.0)
                last = jnp.sum(seen.reshape(-1, 8, 256), axis=0)
                if m == 3:
                    acc[g, :, width - 256 : width] = last
                else:
                    acc[g, :, width - 256 : width] += last
                if m > 0:
                    full = jnp.sum(w[:, : width - 256].reshape(-1, 8, width - 256), axis=0)
                    if m == 3:
                        acc[g, :, : width - 256] = full
                    else:
                        acc[g, :, : width - 256] += full
        rows = [jnp.sum(acc[g], axis=0, keepdims=True) for g in range(4)]
        four = jnp.concatenate(rows, axis=0)
        for src in range(8):
            part[block, src] = four[:, src * TOK : src * TOK + TOK]

    def to_owner(block, row):
        return remote(
            part.at[block, row], abuf.at[z * 8 + y], a_s.at[0], a_r.at[0], device(row, block, c)
        )

    def one_block(turn, carry):
        @pl.when(turn == 1)
        def _():
            advance(2)

        @pl.when(turn == 4)
        def _():
            advance(3)

        @pl.when(turn == 6)
        def _():
            advance(4)

        away = jnp.where(turn == 7, -1, (turn // 2 + 1) * (1 - 2 * (turn % 2)))
        away = jnp.where(turn < 2, turn, away)
        block = (z - away + 8) % 8
        compute(block)

        for row in range(8):

            @pl.when((turn > 0) | (row != y))
            def _():
                to_owner(block, row).start()

        return carry

    lax.fori_loop(0, 8, one_block, 0)

    abuf[z * 8 + y] = part[z, y]

    for step in range(1, 8):
        column(y, (y + step) % 8).wait_send()
    for step in range(1, 4):
        query(mine, (mine + step) % 4).wait_send()
    for m in range(4):
        relay(qbuf.at[m, c], m, c).wait_send()
    for way in range(2):
        for dist in range(1, 5):
            for part_of in range(2):
                if dist < 4 or part_of == way:
                    ring(way, dist, part_of).wait_send()

    others = remote(
        abuf.at[pl.ds(0, 63)], abuf.at[pl.ds(0, 63)], a_s.at[0], a_r.at[0], device(y, z, 1 - c)
    )
    others.wait_recv()
    for h in range(4):
        total = abuf[2 * h] + abuf[2 * h + 1]
        for col in range(1, 8):
            total += abuf[8 * col + 2 * h] + abuf[8 * col + 2 * h + 1]
        o_ref[4 * h : 4 * h + 4, :] = total
    others.wait_send()


def shard(queries, keys, lse, length):
    vmem = pl.BlockSpec(memory_space=pltpu.VMEM)
    dma = pltpu.SemaphoreType.DMA
    return pl.pallas_call(
        kernel,
        out_shape=jax.ShapeDtypeStruct(lse.shape, F32),
        in_specs=[pl.BlockSpec(memory_space=pltpu.SMEM)] + [pl.BlockSpec(memory_space=pl.ANY)] * 3,
        out_specs=vmem,
        scratch_shapes=[
            pltpu.VMEM(queries.shape, BF16),
            pltpu.VMEM(keys.shape, BF16),
            pltpu.VMEM(lse.shape, F32),
            pltpu.VMEM((4, TOK + 16, 256), BF16),
            pltpu.VMEM((4, 64, 128), BF16),
            pltpu.VMEM((NZ, NY, 64, 128), BF16),
            pltpu.VMEM((4, 2, TOK + 16, 256), BF16),
            pltpu.VMEM((4, 4, 2 * TOK, 128), BF16),
            pltpu.VMEM((NY * TOK, 128), BF16),
            pltpu.VMEM((4, 8, NY * TOK), F32),
            pltpu.VMEM((NZ, NY, 4, TOK), F32),
            pltpu.VMEM((NZ * NY, 4, TOK), F32),
            dma((3,)), dma((8,)), dma((8,)), dma((4,)), dma((4,)), dma((4,)), dma((4,)),
            dma((2, 4, 2)), dma((2, 4, 2)), dma((1,)), dma((1,)),
        ],
        compiler_params=pltpu.CompilerParams(
            collective_id=0, has_side_effects=True, vmem_limit_bytes=55224 * 1024
        ),
    )(length, queries, keys, lse)


def solution(mesh):
    both = ("req", "ctx")
    return jax.shard_map(
        shard,
        mesh=mesh,
        in_specs=(P(both, None), P(both, None), P(None, both), P("req")),
        out_specs=P(None, both),
        check_vma=False,
    )
```

```python
import functools

import jax
import jax.numpy as jnp
from jax import lax
from jax.experimental import pallas as pl
from jax.experimental.pallas import tpu as pltpu
from jax.sharding import PartitionSpec as P

HEAD_DIM = 64
TOK = 128
NY, NZ = 8, 8
GROUP = 4
PAST = -30000.0
F32, BF16 = jnp.float32, jnp.bfloat16


def member(half, index):
    return 2 * index + (half + index // 2) % 2


def kernel(
    len_ref, q_hbm, k_hbm, l_hbm, o_ref,
    q_ref, k_ref, l_ref, qsend, kpack, kbuf, qbuf, qaug, kaug, acc, part, abuf,
    in_s, col_s, col_r, q_s, q_r, relay_s, relay_r, ring_s, ring_r, a_s, a_r, right_ok, left_ok,
):
    me = lax.axis_index("ctx")
    y, z, c = me // 16, (me // 2) % 8, me % 2
    half, mine = (y + y // 4) % 2, y // 2

    def device(ty, tz, tc):
        return {"ctx": ty * 16 + tz * 2 + tc}

    def remote(src, dst, send, recv, dev):
        return pltpu.make_async_remote_copy(
            src_ref=src, dst_ref=dst, send_sem=send, recv_sem=recv, device_id=dev
        )

    loads = [
        pltpu.make_async_copy(src, dst, in_s.at[i])
        for i, (src, dst) in enumerate(((k_hbm, k_ref), (l_hbm, l_ref), (q_hbm, q_ref)))
    ]
    for load in loads:
        load.start()
    barrier = pltpu.get_barrier_semaphore()

    def greet(dev):
        pl.semaphore_signal(barrier, inc=1, device_id=dev)

    greet(device(y, z, 1 - c))
    for step in (4, 3, 5, 2, 6, 1, 7):
        greet(device((y + step) % 8, z, c))

    @pl.when(z < 7)
    def _():
        greet(device(y, z + 1, c))

    @pl.when(z == 0)
    def _():
        greet(device(y, 7, c))

    lane64 = lax.broadcasted_iota(jnp.int32, (64, TOK), 1)

    loads[0].wait()

    for pair in range(2):
        two = k_ref[:, pair * 128 : pair * 128 + 128].astype(F32) * HEAD_DIM**-0.5
        top, low = two[:64], two[64:]
        top_r, low_r = pltpu.roll(top, 64, 1), pltpu.roll(low, 64, 1)
        kpack[2 * pair] = jnp.where(lane64 < 64, top, low_r).astype(BF16)
        kpack[2 * pair + 1] = jnp.where(lane64 < 64, top_r, low).astype(BF16)
    kbuf[z, y] = kpack[mine]

    pl.semaphore_wait(barrier, 8 + jnp.where(z > 0, 1, 0) + jnp.where(z == 7, 1, 0))

    @pl.when(z > 0)
    def _():
        pl.semaphore_signal(right_ok, inc=1, device_id=device(y, z - 1, c))

    @pl.when(z == 7)
    def _():
        pl.semaphore_signal(left_ok, inc=1, device_id=device(y, 0, c))

    def column(src_y, dst_y):
        return remote(
            kpack.at[dst_y // 2], kbuf.at[z, src_y], col_s.at[dst_y], col_r.at[src_y],
            device(dst_y, z, c),
        )

    def query(src_m, dst_m):
        return remote(
            qsend.at[dst_m], qbuf.at[src_m, c], q_s.at[dst_m], q_r.at[src_m],
            device(member(half, dst_m), z, c),
        )

    def relay(src, m, core):
        return remote(src, qbuf.at[m, core], relay_s.at[m], relay_r.at[m], device(y, z, 1 - c))

    def ring(way, dist, part_of):
        sign = 1 - 2 * way
        from_dist, hop = (2, 2) if dist == 4 else (dist - 1, 1)
        block = (z - sign * from_dist) % 8
        where = kbuf.at[block, pl.ds(4 * part_of, 4)]
        return remote(
            where, where, ring_s.at[way, dist - 1, part_of], ring_r.at[way, dist - 1, part_of],
            device(y, (z + hop * sign) % 8, c),
        )

    for step in (4, 3, 5, 2, 6, 1, 7):
        column(y, (y + step) % 8).start()
    loads[1].wait()
    loads[2].wait()
    position = me * TOK + lax.broadcasted_iota(jnp.int32, (16, TOK), 1)
    neg = jnp.where(position < len_ref[0], -l_ref[...], PAST)
    hi = neg.astype(BF16).astype(F32)
    mid = (neg - hi).astype(BF16).astype(F32)
    low = neg - hi - mid
    for head in range(4):
        rows = slice(4 * head, 4 * head + 4)
        parts = jnp.concatenate(
            [hi[rows], mid[rows], low[rows], jnp.zeros((4, TOK), F32)], axis=0
        )
        qsend[head, :TOK, :] = q_ref[:, head * 256 : head * 256 + 256]
        qsend[head, TOK:, :] = jnp.concatenate([parts, parts], axis=1).astype(BF16)

    own = relay(qsend.at[mine], mine, c)
    own.start()
    for step in range(1, 4):
        query(mine, (mine + step) % 4).start()
    qbuf[mine, c] = qsend[mine]

    for part_of in range(2):
        for src in range(4 * part_of, 4 * part_of + 4):

            @pl.when(src != y)
            def _():
                column(src, y).wait_recv()

        if part_of == 0:

            @pl.when(z < 7)
            def _():
                pl.semaphore_wait(right_ok, 1)

        ring(0, 1, part_of).start()

    @pl.when(z == 0)
    def _():
        pl.semaphore_wait(left_ok, 1)

    for part_of in range(2):
        ring(1, 1, part_of).start()

    def advance(dist):
        for part_of in range(2):
            for way in range(2):
                if dist < 4 or part_of == way:
                    ring(way, dist, part_of).wait_recv()
            for way in range(2):
                if dist < 3:
                    ring(way, dist + 1, part_of).start()
                if dist == 2 and part_of == way:
                    ring(way, 4, part_of).start()

    lane = lax.broadcasted_iota(jnp.int32, (TOK, TOK), 1)

    def prepare(m, core):
        tail = qbuf[m, core, TOK:, :TOK].astype(F32)
        cols = jnp.concatenate(
            [jnp.zeros((64, TOK), F32), tail, jnp.zeros((48, TOK), F32)], axis=0
        ).T
        for pair in range(2):
            two = qbuf[m, core, :TOK, pair * 128 : pair * 128 + 128].astype(F32)
            for odd in range(2):
                g = 2 * pair + odd
                head = pltpu.roll(two, 64, 1) if odd else two
                keep = (lane >= 64) & (lane % 4 == g)
                value = jnp.where(lane < 64, head, jnp.where(keep, cols, 0.0))
                qaug[m, g, pl.ds(core * TOK, TOK), :] = value.astype(BF16)

    prepare(mine, c)
    relay(qbuf.at[mine, 1 - c], mine, 1 - c).wait_recv()
    prepare(mine, 1 - c)
    advance(1)
    for step in range(1, 4):
        src = (mine - step) % 4
        query(src, mine).wait_recv()
        relay(qbuf.at[src, c], src, c).start()
        prepare(src, c)
    for step in range(1, 4):
        src = (mine - step) % 4
        relay(qbuf.at[src, 1 - c], src, 1 - c).wait_recv()
        prepare(src, 1 - c)

    tokens = lax.broadcasted_iota(jnp.int32, (2 * TOK, 2 * TOK), 0)
    key_of = lax.broadcasted_iota(jnp.int32, (1, 2 * TOK), 1)

    def compute(block):
        for src in range(8):
            packed = kbuf[block, src].astype(F32)
            tail = jnp.where(lane64 < 76, 1.0, 0.0)
            at = src * TOK
            kaug[at : at + 64, :] = jnp.where(lane64 < 64, packed, tail).astype(BF16)
            kaug[at + 64 : at + 128, :] = jnp.where(
                lane64 < 64, pltpu.roll(packed, 64, 1), tail
            ).astype(BF16)
        for m in range(3, -1, -1):
            width = 256 * (m + 1)
            key_at = ((2 * m + key_of // TOK) * NZ + block) * 2 * TOK + c * TOK + key_of % TOK
            first = key_at - (member(half, m) * NZ + z) * 2 * TOK
            for g in range(4):
                w = jnp.exp(
                    lax.dot_general(
                        qaug[m, g], kaug[:width, :], (((1,), (1,)), ((), ())),
                        preferred_element_type=F32,
                    )
                )
                seen = jnp.where(tokens >= first, w[:, width - 256 :], 0.0)
                last = jnp.sum(seen.reshape(-1, 8, 256), axis=0)
                if m == 3:
                    acc[g, :, width - 256 : width] = last
                else:
                    acc[g, :, width - 256 : width] += last
                if m > 0:
                    full = jnp.sum(w[:, : width - 256].reshape(-1, 8, width - 256), axis=0)
                    if m == 3:
                        acc[g, :, : width - 256] = full
                    else:
                        acc[g, :, : width - 256] += full
        rows = [jnp.sum(acc[g], axis=0, keepdims=True) for g in range(4)]
        four = jnp.concatenate(rows, axis=0)
        for src in range(8):
            part[block, src] = four[:, src * TOK : src * TOK + TOK]

    def to_owner(block, row):
        return remote(
            part.at[block, row], abuf.at[z * 8 + y], a_s.at[0], a_r.at[0], device(row, block, c)
        )

    def one_block(turn, carry):
        @pl.when(turn == 1)
        def _():
            advance(2)

        @pl.when(turn == 5)
        def _():
            advance(4)
            advance(3)

        away = ((turn + 1) // 2) * (2 * (turn % 2) - 1)
        away = jnp.where(turn < 5, away, jnp.where(turn == 5, 4, 3 - 6 * (turn - 6)))
        block = (z - away + 8) % 8
        compute(block)

        for row in range(8):

            @pl.when((turn > 0) | (row != y))
            def _():
                to_owner(block, row).start()

        return carry

    lax.fori_loop(0, 8, one_block, 0)

    abuf[z * 8 + y] = part[z, y]

    for step in range(1, 8):
        column(y, (y + step) % 8).wait_send()
    for step in range(1, 4):
        query(mine, (mine + step) % 4).wait_send()
    for m in range(4):
        relay(qbuf.at[m, c], m, c).wait_send()
    for way in range(2):
        for dist in range(1, 5):
            for part_of in range(2):
                if dist < 4 or part_of == way:
                    ring(way, dist, part_of).wait_send()

    others = remote(
        abuf.at[pl.ds(0, 63)], abuf.at[pl.ds(0, 63)], a_s.at[0], a_r.at[0], device(y, z, 1 - c)
    )
    others.wait_recv()
    for h in range(4):
        total = abuf[2 * h] + abuf[2 * h + 1]
        for col in range(1, 8):
            total += abuf[8 * col + 2 * h] + abuf[8 * col + 2 * h + 1]
        o_ref[4 * h : 4 * h + 4, :] = total
    others.wait_send()


def shard(queries, keys, lse, length):
    vmem = pl.BlockSpec(memory_space=pltpu.VMEM)
    dma = pltpu.SemaphoreType.DMA
    return pl.pallas_call(
        kernel,
        out_shape=jax.ShapeDtypeStruct(lse.shape, F32),
        in_specs=[pl.BlockSpec(memory_space=pltpu.SMEM)] + [pl.BlockSpec(memory_space=pl.ANY)] * 3,
        out_specs=vmem,
        scratch_shapes=[
            pltpu.VMEM(queries.shape, BF16),
            pltpu.VMEM(keys.shape, BF16),
            pltpu.VMEM(lse.shape, F32),
            pltpu.VMEM((4, TOK + 16, 256), BF16),
            pltpu.VMEM((4, 64, 128), BF16),
            pltpu.VMEM((NZ, NY, 64, 128), BF16),
            pltpu.VMEM((4, 2, TOK + 16, 256), BF16),
            pltpu.VMEM((4, 4, 2 * TOK, 128), BF16),
            pltpu.VMEM((NY * TOK, 128), BF16),
            pltpu.VMEM((4, 8, NY * TOK), F32),
            pltpu.VMEM((NZ, NY, 4, TOK), F32),
            pltpu.VMEM((NZ * NY, 4, TOK), F32),
            dma((3,)), dma((8,)), dma((8,)), dma((4,)), dma((4,)), dma((4,)), dma((4,)),
            dma((2, 4, 2)), dma((2, 4, 2)), dma((1,)), dma((1,)),
            pltpu.SemaphoreType.REGULAR, pltpu.SemaphoreType.REGULAR,
        ],
        compiler_params=pltpu.CompilerParams(
            collective_id=0, has_side_effects=True, vmem_limit_bytes=55224 * 1024
        ),
    )(length, queries, keys, lse)


def solution(mesh):
    both = ("req", "ctx")
    return jax.shard_map(
        shard,
        mesh=mesh,
        in_specs=(P(both, None), P(both, None), P(None, both), P("req")),
        out_specs=P(None, both),
        check_vma=False,
    )
```

```python
import functools

import jax
import jax.numpy as jnp
from jax import lax
from jax.experimental import pallas as pl
from jax.experimental.pallas import tpu as pltpu
from jax.sharding import PartitionSpec as P

HEAD_DIM = 64
TOK = 128
NY, NZ = 8, 8
GROUP = 4
PAST = -30000.0
F32, BF16 = jnp.float32, jnp.bfloat16


def member(half, index):
    return 2 * index + (half + index // 2) % 2


def kernel(
    len_ref, q_hbm, k_hbm, l_hbm, o_ref,
    q_ref, k_ref, l_ref, qsend, kpack, kbuf, qbuf, qaug, kaug, acc, part, abuf,
    in_s, col_s, col_r, q_s, q_r, relay_s, relay_r, ring_s, ring_r, a_s, a_r, right_ok, left_ok,
):
    me = lax.axis_index("ctx")
    y, z, c = me // 16, (me // 2) % 8, me % 2
    half, mine = (y + y // 4) % 2, y // 2

    def device(ty, tz, tc):
        return {"ctx": ty * 16 + tz * 2 + tc}

    def remote(src, dst, send, recv, dev):
        return pltpu.make_async_remote_copy(
            src_ref=src, dst_ref=dst, send_sem=send, recv_sem=recv, device_id=dev
        )

    loads = [
        pltpu.make_async_copy(src, dst, in_s.at[i])
        for i, (src, dst) in enumerate(((k_hbm, k_ref), (l_hbm, l_ref), (q_hbm, q_ref)))
    ]
    for load in loads:
        load.start()
    barrier = pltpu.get_barrier_semaphore()

    def greet(dev):
        pl.semaphore_signal(barrier, inc=1, device_id=dev)

    greet(device(y, z, 1 - c))
    for step in (4, 3, 5, 2, 6, 1, 7):
        greet(device((y + step) % 8, z, c))

    @pl.when(z < 7)
    def _():
        greet(device(y, z + 1, c))

    @pl.when(z == 0)
    def _():
        greet(device(y, 7, c))

    lane64 = lax.broadcasted_iota(jnp.int32, (64, TOK), 1)

    loads[0].wait()

    for pair in range(2):
        two = k_ref[:, pair * 128 : pair * 128 + 128].astype(F32) * HEAD_DIM**-0.5
        top, low = two[:64], two[64:]
        top_r, low_r = pltpu.roll(top, 64, 1), pltpu.roll(low, 64, 1)
        kpack[2 * pair] = jnp.where(lane64 < 64, top, low_r).astype(BF16)
        kpack[2 * pair + 1] = jnp.where(lane64 < 64, top_r, low).astype(BF16)
    kbuf[z, y] = kpack[mine]

    pl.semaphore_wait(barrier, 8 + jnp.where(z > 0, 1, 0) + jnp.where(z == 7, 1, 0))

    @pl.when(z > 0)
    def _():
        pl.semaphore_signal(right_ok, inc=1, device_id=device(y, z - 1, c))

    @pl.when(z == 7)
    def _():
        pl.semaphore_signal(left_ok, inc=1, device_id=device(y, 0, c))

    def column(src_y, dst_y):
        return remote(
            kpack.at[dst_y // 2], kbuf.at[z, src_y], col_s.at[dst_y], col_r.at[src_y],
            device(dst_y, z, c),
        )

    def query(src_m, dst_m):
        return remote(
            qsend.at[dst_m], qbuf.at[src_m, c], q_s.at[dst_m], q_r.at[src_m],
            device(member(half, dst_m), z, c),
        )

    def relay(src, m, core):
        return remote(src, qbuf.at[m, core], relay_s.at[m], relay_r.at[m], device(y, z, 1 - c))

    def ring(way, dist, part_of):
        sign = 1 - 2 * way
        from_dist, hop = (2, 2) if dist == 4 else (dist - 1, 1)
        block = (z - sign * from_dist) % 8
        where = kbuf.at[block, pl.ds(4 * part_of, 4)]
        return remote(
            where, where, ring_s.at[way, dist - 1, part_of], ring_r.at[way, dist - 1, part_of],
            device(y, (z + hop * sign) % 8, c),
        )

    for step in (4, 3, 5, 2, 6, 1, 7):
        column(y, (y + step) % 8).start()
    loads[1].wait()
    loads[2].wait()
    position = me * TOK + lax.broadcasted_iota(jnp.int32, (16, TOK), 1)
    neg = jnp.where(position < len_ref[0], -l_ref[...], PAST)
    hi = neg.astype(BF16).astype(F32)
    mid = (neg - hi).astype(BF16).astype(F32)
    low = neg - hi - mid
    for head in range(4):
        rows = slice(4 * head, 4 * head + 4)
        parts = jnp.concatenate(
            [hi[rows], mid[rows], low[rows], jnp.zeros((4, TOK), F32)], axis=0
        )
        qsend[head, :TOK, :] = q_ref[:, head * 256 : head * 256 + 256]
        qsend[head, TOK:, :] = jnp.concatenate([parts, parts], axis=1).astype(BF16)

    own = relay(qsend.at[mine], mine, c)
    own.start()
    for step in range(1, 4):
        query(mine, (mine + step) % 4).start()
    qbuf[mine, c] = qsend[mine]

    for part_of in range(2):
        for src in range(4 * part_of, 4 * part_of + 4):

            @pl.when(src != y)
            def _():
                column(src, y).wait_recv()

        if part_of == 0:

            @pl.when(z < 7)
            def _():
                pl.semaphore_wait(right_ok, 1)

        ring(0, 1, part_of).start()

    @pl.when(z == 0)
    def _():
        pl.semaphore_wait(left_ok, 1)

    for part_of in range(2):
        ring(1, 1, part_of).start()

    def advance(dist):
        for part_of in range(2):
            for way in range(2):
                if dist < 4 or part_of == way:
                    ring(way, dist, part_of).wait_recv()
            for way in range(2):
                if dist < 3:
                    ring(way, dist + 1, part_of).start()
                if dist == 2 and part_of == way:
                    ring(way, 4, part_of).start()

    lane = lax.broadcasted_iota(jnp.int32, (TOK, TOK), 1)

    def prepare(m, core):
        tail = qbuf[m, core, TOK:, :TOK].astype(F32)
        cols = jnp.concatenate(
            [jnp.zeros((64, TOK), F32), tail, jnp.zeros((48, TOK), F32)], axis=0
        ).T
        for pair in range(2):
            two = qbuf[m, core, :TOK, pair * 128 : pair * 128 + 128].astype(F32)
            for odd in range(2):
                g = 2 * pair + odd
                head = pltpu.roll(two, 64, 1) if odd else two
                keep = (lane >= 64) & (lane % 4 == g)
                value = jnp.where(lane < 64, head, jnp.where(keep, cols, 0.0))
                qaug[m, g, pl.ds(core * TOK, TOK), :] = value.astype(BF16)

    prepare(mine, c)
    relay(qbuf.at[mine, 1 - c], mine, 1 - c).wait_recv()
    prepare(mine, 1 - c)
    advance(1)
    for step in range(1, 4):
        src = (mine - step) % 4
        query(src, mine).wait_recv()
        relay(qbuf.at[src, c], src, c).start()
        prepare(src, c)
    for step in range(1, 4):
        src = (mine - step) % 4
        relay(qbuf.at[src, 1 - c], src, 1 - c).wait_recv()
        prepare(src, 1 - c)

    tokens = lax.broadcasted_iota(jnp.int32, (2 * TOK, 2 * TOK), 0)
    key_of = lax.broadcasted_iota(jnp.int32, (1, 2 * TOK), 1)

    def compute(block, own):
        for src in range(8):
            packed = kbuf[block, src].astype(F32)
            tail = jnp.where(lane64 < 76, 1.0, 0.0)
            at = src * TOK
            kaug[at : at + 64, :] = jnp.where(lane64 < 64, packed, tail).astype(BF16)
            kaug[at + 64 : at + 128, :] = jnp.where(
                lane64 < 64, pltpu.roll(packed, 64, 1), tail
            ).astype(BF16)
        for m in range(3, -1, -1):
            width = 256 * (m + 1)
            key_at = ((2 * m + key_of // TOK) * NZ + block) * 2 * TOK + c * TOK + key_of % TOK
            first = key_at - (member(half, m) * NZ + z) * 2 * TOK
            for g in range(4):
                w = jnp.exp(
                    lax.dot_general(
                        qaug[m, g], kaug[:width, :], (((1,), (1,)), ((), ())),
                        preferred_element_type=F32,
                    )
                )
                last = w[:, width - 256 :]
                if own:
                    last = jnp.where(tokens >= first, last, 0.0)
                last = jnp.sum(last.reshape(-1, 8, 256), axis=0)
                if not own:
                    last = jnp.where(first <= 0, last, 0.0)
                if m == 3:
                    acc[g, :, width - 256 : width] = last
                else:
                    acc[g, :, width - 256 : width] += last
                if m > 0:
                    full = jnp.sum(w[:, : width - 256].reshape(-1, 8, width - 256), axis=0)
                    if m == 3:
                        acc[g, :, : width - 256] = full
                    else:
                        acc[g, :, : width - 256] += full
        rows = [jnp.sum(acc[g], axis=0, keepdims=True) for g in range(4)]
        four = jnp.concatenate(rows, axis=0)
        for src in range(8):
            part[block, src] = four[:, src * TOK : src * TOK + TOK]

    def to_owner(block, row):
        return remote(
            part.at[block, row], abuf.at[z * 8 + y], a_s.at[0], a_r.at[0], device(row, block, c)
        )

    def one_block(turn, carry):
        @pl.when(turn == 1)
        def _():
            advance(2)

        @pl.when(turn == 5)
        def _():
            advance(4)
            advance(3)

        away = ((turn + 1) // 2) * (2 * (turn % 2) - 1)
        away = jnp.where(turn < 5, away, jnp.where(turn == 5, 4, 3 - 6 * (turn - 6)))
        block = (z - away + 8) % 8
        compute(block, False)

        for row in range(8):
            to_owner(block, row).start()

        return carry

    compute(z, True)
    for step in range(1, 8):
        to_owner(z, (y + step) % 8).start()
    lax.fori_loop(1, 8, one_block, 0)

    abuf[z * 8 + y] = part[z, y]

    for step in range(1, 8):
        column(y, (y + step) % 8).wait_send()
    for step in range(1, 4):
        query(mine, (mine + step) % 4).wait_send()
    for m in range(4):
        relay(qbuf.at[m, c], m, c).wait_send()
    for way in range(2):
        for dist in range(1, 5):
            for part_of in range(2):
                if dist < 4 or part_of == way:
                    ring(way, dist, part_of).wait_send()

    others = remote(
        abuf.at[pl.ds(0, 63)], abuf.at[pl.ds(0, 63)], a_s.at[0], a_r.at[0], device(y, z, 1 - c)
    )
    others.wait_recv()
    for h in range(4):
        total = abuf[2 * h] + abuf[2 * h + 1]
        for col in range(1, 8):
            total += abuf[8 * col + 2 * h] + abuf[8 * col + 2 * h + 1]
        o_ref[4 * h : 4 * h + 4, :] = total
    others.wait_send()


def shard(queries, keys, lse, length):
    vmem = pl.BlockSpec(memory_space=pltpu.VMEM)
    dma = pltpu.SemaphoreType.DMA
    return pl.pallas_call(
        kernel,
        out_shape=jax.ShapeDtypeStruct(lse.shape, F32),
        in_specs=[pl.BlockSpec(memory_space=pltpu.SMEM)] + [pl.BlockSpec(memory_space=pl.ANY)] * 3,
        out_specs=vmem,
        scratch_shapes=[
            pltpu.VMEM(queries.shape, BF16),
            pltpu.VMEM(keys.shape, BF16),
            pltpu.VMEM(lse.shape, F32),
            pltpu.VMEM((4, TOK + 16, 256), BF16),
            pltpu.VMEM((4, 64, 128), BF16),
            pltpu.VMEM((NZ, NY, 64, 128), BF16),
            pltpu.VMEM((4, 2, TOK + 16, 256), BF16),
            pltpu.VMEM((4, 4, 2 * TOK, 128), BF16),
            pltpu.VMEM((NY * TOK, 128), BF16),
            pltpu.VMEM((4, 8, NY * TOK), F32),
            pltpu.VMEM((NZ, NY, 4, TOK), F32),
            pltpu.VMEM((NZ * NY, 4, TOK), F32),
            dma((3,)), dma((8,)), dma((8,)), dma((4,)), dma((4,)), dma((4,)), dma((4,)),
            dma((2, 4, 2)), dma((2, 4, 2)), dma((1,)), dma((1,)),
            pltpu.SemaphoreType.REGULAR, pltpu.SemaphoreType.REGULAR,
        ],
        compiler_params=pltpu.CompilerParams(
            collective_id=0, has_side_effects=True, vmem_limit_bytes=55224 * 1024
        ),
    )(length, queries, keys, lse)


def solution(mesh):
    both = ("req", "ctx")
    return jax.shard_map(
        shard,
        mesh=mesh,
        in_specs=(P(both, None), P(both, None), P(None, both), P("req")),
        out_specs=P(None, both),
        check_vma=False,
    )
```
